32 devices in a mesh: row: 16 (over z, y, x), col: 2 (over core).
Axes of the slice: x: 2, y: 2, z: 4, core: 2. Of those that a mesh axis runs over, the one named last changes fastest.
Arguments:
- w_integral: bfloat16 [38400, 4800], P('row', 'col'), may hold values from -0.125 to 0.125
- amplitudes: bfloat16 [4800, 4800], P('row', 'col'), may hold values from -6 to 6
- task_tiles: int32 [16, 7], P('row'), may hold values from -1 to 7, as said below
Outputs:
- residual: bfloat16 [38400, 4800], P('row', 'col')
The draws below stay inside these ranges and needn't reach their ends.
Inputs may be any that keep to these rules, and one draw needn't show every extreme that they name: `task_tiles`: in each row block the live entries come first, name distinct contraction tiles, and number 1 to 7; the remaining entries are -1. Some row block has 7 live entries, and row blocks 2 m and 2 m + 1 together have exactly 8.
All inputs are finite; a program needn't handle non-finite values.
Results may differ from the reference program's by a relative error of at most 0.001.
Values may be sent and summed in bfloat16 or wider, within the bound.
A program may use at most 128 MiB of HBM per device.

```python
import jax
import jax.numpy as jnp

TILE = 24
OCC_BLK = 25
MOST = 7
PAIR = 8
KT = 8
KTS = 600
ROWS = 38400
KCON = 4800
COLS = 4800
ROW_BLOCKS = 16


def order_tiles(sub_key):
    return jax.random.permutation(sub_key, KT)


def draw_task_tiles(key, part):
    key_count, key_force, key_flip, key_order = jax.random.split(key, 4)
    pair_count = ROW_BLOCKS // 2
    leading = jax.random.randint(key_count, (pair_count,), PAIR - MOST, MOST + 1)
    forced = jax.random.randint(key_force, (), 0, pair_count)
    leading = jnp.where(jnp.arange(pair_count) == forced, MOST, leading)
    flipped = jax.random.randint(key_flip, (pair_count,), 0, 2)
    even_count = jnp.where(flipped == 1, PAIR - leading, leading)
    counts_all = jnp.stack([even_count, PAIR - even_count], axis=1).reshape(ROW_BLOCKS)
    orders = jax.vmap(order_tiles)(jax.random.split(key_order, ROW_BLOCKS))
    slot_index = jnp.arange(MOST)
    chosen = jnp.where(slot_index[None, :] < counts_all[:, None], orders[:, :MOST], -1)
    return chosen.astype(jnp.int32)


def levels(stream_key, dims, pieces, smallest, top_value):
    gain, own = 1.0, jax.random.fold_in(stream_key, 6)
    for dim, blocks in pieces:
        draws = jnp.exp(jax.random.uniform(jax.random.fold_in(own, dim), (blocks,), jnp.float32, smallest / len(pieces), top_value / len(pieces)))
        gain = gain * jnp.repeat(draws, dims[dim] // blocks).reshape([-1 if axis == dim else 1 for axis in range(len(dims))])
    return gain


def bell_draw(own_key, dims, spread, most, cuts=(), kind=jnp.bfloat16):
    factor_of = levels(own_key, dims, cuts, -0.22, 0.18) if cuts else 1.0
    result = jax.random.normal(own_key, dims, jnp.float32) * spread * factor_of
    return jnp.minimum(jnp.maximum(result, -most), most).astype(kind)


def setup_inputs(seed: int = 0) -> dict:
    seeds = jax.random.split(jax.random.key(seed), 4)
    return {
        "w_integral": bell_draw(seeds[0], (ROWS, KCON), (4 * KTS) ** -0.5, 0.125, ((0, 16), (1, 2))),
        "amplitudes": bell_draw(seeds[1], (KCON, COLS), 1.0, 6.0, ((0, 16), (1, 2))),
        "task_tiles": draw_task_tiles(jax.random.fold_in(seeds[3], 71), 0),
    }


def reference(w_integral, amplitudes, task_tiles):
    tile_ids = jnp.arange(KT, dtype=jnp.int32)
    live = jnp.sum((task_tiles[:, :, None] == tile_ids[None, None, :]).astype(jnp.int32), axis=1)
    block_rows = ROWS // ROW_BLOCKS
    tile_width = OCC_BLK * TILE
    shaped = w_integral.reshape(ROW_BLOCKS, block_rows, KT, tile_width)
    masked = shaped * live[:, None, :, None].astype(w_integral.dtype)
    cycle_term = jnp.dot(masked.reshape(ROWS, KCON), amplitudes, preferred_element_type=jnp.float32)
    return cycle_term.astype(jnp.bfloat16)
```

```python
import functools

import jax
import jax.numpy as jnp
from jax import lax
from jax.experimental import pallas as pl
from jax.experimental.pallas import tpu as pltpu
from jax.sharding import PartitionSpec as P

KT = 8
PIECES = 6
MESH = pl.DeviceIdType.MESH
XD, YD, ZUP, ZDN = 0, 1, 2, 3


def kernel(n, cols, cfg, w_ref, t_ref, live_ref, out_ref, wt_ref,
           tbuf, acc, win, wout, wbuf, obuf,
           recv_sem, send_sem, own_sem, win_sem, wl_sem, ws_sem, wr_sem, wb_sem, o_sem):
    rows, kw, width, kshard, spad, group, chunk, bounds, splits = cfg
    nchunk = rows // chunk
    tiles = kw // (kshard * group)
    zs_count = n // 4
    me = lax.axis_index("row")
    col = lax.axis_index("col")
    x = lax.rem(me, 2)
    y = lax.rem(me // 2, 2)
    z = me // 4
    xo, yo = 1 - x, 1 - y
    far = jnp.where(2 * z < zs_count, zs_count - 1, 0)

    def idx(zz, yy, xx):
        return (zz * 2 + yy) * 2 + xx

    target = [(idx(z, y, xo), col), (idx(z, yo, x), col),
              (idx(z + 1, y, x), col), (idx(z - 1, y, x), col)]
    has_up, has_dn = z + 1 < zs_count, z > 0

    barrier = pltpu.get_barrier_semaphore()

    def greet(dev):
        pl.semaphore_signal(barrier, inc=1, device_id=dev, device_id_type=MESH)

    greet(target[XD])
    greet(target[YD])
    pl.when(has_up)(lambda: greet(target[ZUP]))
    pl.when(has_dn)(lambda: greet(target[ZDN]))
    for o in range(1, cols):
        greet((me, lax.rem(col + o, cols)))
    heard = 1 + cols + jnp.where(has_up, 1, 0) + jnp.where(has_dn, 1, 0)
    own = pltpu.make_async_copy(t_ref, tbuf.at[me], own_sem)
    own.start()
    own.wait()
    pl.semaphore_wait(barrier, heard)

    def piece(shard, p):
        return tbuf.at[shard, pl.ds(bounds[p], bounds[p + 1] - bounds[p])]

    def remote(link, shard, p):
        return pltpu.make_async_remote_copy(
            src_ref=piece(shard, p), dst_ref=piece(shard, p),
            send_sem=send_sem.at[link, shard, p], recv_sem=recv_sem.at[shard, p],
            device_id=target[link], device_id_type=MESH)

    def send(go, link, shard, p):
        if go:
            remote(link, shard, p).start()
        else:
            remote(link, shard, p).wait_send()

    def arrive(go, shard, p):
        if go:
            remote(XD, shard, p).wait_recv()

    half = PIECES // 2
    via_z = list(range(1, PIECES - 1))
    via_x, via_y = PIECES - 1, 0

    def own_stage(go):
        for p in range(PIECES):
            send(go, XD, me, p)
            send(go, YD, me, p)
            pl.when(has_up)(functools.partial(send, go, ZUP, me, p))
            pl.when(has_dn)(functools.partial(send, go, ZDN, me, p))

    def onward(go, d, shard, p):
        pl.when((d > 0) & has_dn)(functools.partial(send, go, ZDN, shard, p))
        pl.when((d < 0) & has_up)(functools.partial(send, go, ZUP, shard, p))

    def both(k, work):
        def step(i, carry):
            d = 1 - 2 * i
            zz = z + d * k

            @pl.when((zz >= 0) & (zz < zs_count))
            def _():
                work(d, zz)
            return carry
        lax.fori_loop(0, 2, step, 0)

    def line_stage(go, k):
        def work(d, zz):
            s = idx(zz, y, x)
            for p in range(PIECES):
                arrive(go, s, p)
                onward(go, d, s, p)
                send(go, XD, s, p)
                send(go, YD, s, p)
        both(k, work)

    def diag_stage(go, k):
        def work(d, zz):
            s = idx(zz, yo, xo)
            for p in via_z:
                arrive(go, s, p)
                onward(go, d, s, p)
        both(k, work)

    def side(go, zz, to_y, to_x):
        sx, sy = idx(zz, y, xo), idx(zz, yo, x)
        for p in range(PIECES):
            arrive(go, sx, p)
            if p in to_y:
                send(go, YD, sx, p)
            arrive(go, sy, p)
            if p in to_x:
                send(go, XD, sy, p)

    def side_stage(go, k):
        both(k, lambda d, zz: side(go, zz, (via_y,), (via_x,)))

    def diag_home(go):
        s = idx(z, yo, xo)
        for p in range(PIECES):
            arrive(go, s, p)
            if p in via_z:
                pl.when(has_up)(functools.partial(send, go, ZUP, s, p))
                pl.when(has_dn)(functools.partial(send, go, ZDN, s, p))

    home = (tuple(range(half)), tuple(range(half, PIECES)))

    own_stage(True)

    wout[...] = jnp.zeros_like(wout)

    def w_in(c, slot):
        return pltpu.make_async_copy(w_ref.at[pl.ds(c * chunk, chunk)], win.at[slot], win_sem.at[slot])

    def w_dst(c, owner):
        return wt_ref.at[pl.ds(owner * tiles, tiles), pl.ds(c * chunk, chunk)]

    def w_local(c, slot):
        return pltpu.make_async_copy(wout.at[slot], w_dst(c, col), wl_sem.at[slot])

    def w_remote(c, slot, o):
        return pltpu.make_async_remote_copy(
            src_ref=wout.at[slot], dst_ref=w_dst(c, col),
            send_sem=ws_sem.at[slot, o], recv_sem=wr_sem.at[c, o],
            device_id=(me, lax.rem(col + o, cols)), device_id_type=MESH)

    def w_drain(c, slot):
        w_local(c, slot).wait()
        for o in range(1, cols):
            w_remote(c, slot, o).wait_send()

    w_in(0, 0).start()

    def w_step(c, carry):
        slot = lax.rem(c, 2)
        pl.when(c + 1 < nchunk)(lambda: w_in(c + 1, 1 - slot).start())
        w_in(c, slot).wait()
        pl.when(c >= 2)(lambda: w_drain(c - 2, slot))
        for j in range(tiles):
            for g in range(group):
                at = (j * group + g) * kshard
                wout[slot, j, :, g * spad:g * spad + kshard] = win[slot, :, at:at + kshard]
        w_local(c, slot).start()
        for o in range(1, cols):
            w_remote(c, slot, o).start()
        return carry

    lax.fori_loop(0, nchunk, w_step, 0)

    def w_wait():
        for c in range(max(0, nchunk - 2), nchunk):
            w_drain(c, c % 2)

        def step(c, carry):
            for o in range(1, cols):
                pltpu.make_async_remote_copy(
                    src_ref=wout.at[0], dst_ref=w_dst(c, lax.rem(col + cols - o, cols)),
                    send_sem=ws_sem.at[0, o], recv_sem=wr_sem.at[c, o],
                    device_id=(me, lax.rem(col + o, cols)), device_id_type=MESH).wait_recv()
            return carry
        lax.fori_loop(0, nchunk, step, 0)

    def product(first_shard, kind):
        t = first_shard // group
        live = live_ref[t]

        def fetch(c, slot):
            return pltpu.make_async_copy(wt_ref.at[t, pl.ds(c * chunk, chunk)], wbuf.at[slot], wb_sem.at[slot])

        def store(c, slot):
            return pltpu.make_async_copy(obuf.at[slot], out_ref.at[pl.ds(c * chunk, chunk)], o_sem.at[slot])

        fetch(0, 0).start()

        def step(c, carry):
            slot = lax.rem(c, 2)
            pl.when(c + 1 < nchunk)(lambda: fetch(c + 1, 1 - slot).start())
            fetch(c, slot).wait()
            if kind == "last":
                pl.when(c >= 2)(lambda: store(c - 2, slot).wait())
            a = wbuf[slot]
            at = pl.ds(pl.multiple_of(c * chunk, 16), chunk)
            for lo, hi in splits:
                b = tbuf[pl.ds(t * group, group), :, lo:hi].reshape(group * spad, hi - lo)
                d = jnp.dot(a, b, preferred_element_type=jnp.float32) * live
                if kind == "first":
                    acc[at, lo:hi] = d
                elif kind == "last":
                    obuf[slot, :, lo:hi] = (acc[at, lo:hi] + d).astype(jnp.bfloat16)
                else:
                    acc[at, lo:hi] += d
            if kind == "last":
                store(c, slot).start()
            return carry

        lax.fori_loop(0, nchunk, step, 0)
        if kind == "last":
            for c in range(max(0, nchunk - 2), nchunk):
                store(c, c % 2).wait()

    pair = group == 2

    line_stage(True, 1)
    side(True, z, *home)
    w_wait()
    if pair:
        product(idx(z, y, 0), "first")
        diag_home(True)
        product(idx(z, yo, 0), "add")
    else:
        diag_home(True)
        product(idx(z, 0, 0), "first")

    def loop(k, carry):
        line_stage(True, k)
        diag_stage(True, k - 1)
        side_stage(True, k - 1)

        def finish(d, zz):
            if pair:
                product(idx(zz, y, 0), "add")
            s = idx(zz, yo, xo)
            for p in (via_x, via_y):
                arrive(True, s, p)

            @pl.when(zz != far)
            def _():
                product(idx(zz, yo if pair else 0, 0), "add")
        both(k - 1, finish)
        return carry

    lax.fori_loop(2, zs_count + 1, loop, 0)
    product(idx(far, yo if pair else 0, 0), "last")

    own_stage(False)
    side(False, z, *home)
    diag_home(False)

    def drain(k, carry):
        line_stage(False, k)
        diag_stage(False, k)
        side_stage(False, k)
        return carry
    lax.fori_loop(1, zs_count, drain, 0)


def body(n, cols, w, t, task_tiles):
    rows, kw = w.shape
    kshard, width = t.shape
    depth = kshard * n // KT
    group = depth // kshard
    spad = -(-kshard // 16) * 16
    chunk = max(c for c in range(16, min(rows, 240) + 1, 16) if rows % c == 0)
    units = spad // 16
    bounds = tuple(units * p // PIECES * 16 for p in range(PIECES + 1))
    parts = max(1, width // 768)
    edges = [768 * i for i in range(parts)] + [width]
    splits = tuple(zip(edges[:-1], edges[1:]))
    tiles = kw // depth
    nchunk = rows // chunk
    tile_ids = jnp.arange(KT, dtype=jnp.int32)
    live = jnp.sum((task_tiles[0][:, None] == tile_ids[None, :]).astype(jnp.int32), axis=0)
    t = jnp.pad(t, ((0, spad - kshard), (0, 0)))
    cfg = (rows, kw, width, kshard, spad, group, chunk, bounds, splits)
    any_space = pl.BlockSpec(memory_space=pl.ANY)
    bf16 = jnp.bfloat16
    out, _ = pl.pallas_call(
        functools.partial(kernel, n, cols, cfg),
        out_shape=(jax.ShapeDtypeStruct((rows, width), bf16),
                   jax.ShapeDtypeStruct((KT, rows, group * spad), bf16)),
        in_specs=[any_space, any_space, pl.BlockSpec(memory_space=pltpu.SMEM)],
        out_specs=(any_space, any_space),
        scratch_shapes=[
            pltpu.VMEM((n, spad, width), bf16),
            pltpu.VMEM((rows, width), jnp.float32),
            pltpu.VMEM((2, chunk, kw), bf16),
            pltpu.VMEM((2, tiles, chunk, group * spad), bf16),
            pltpu.VMEM((2, chunk, group * spad), bf16),
            pltpu.VMEM((2, chunk, width), bf16),
            pltpu.SemaphoreType.DMA((n, PIECES)),
            pltpu.SemaphoreType.DMA((4, n, PIECES)),
            pltpu.SemaphoreType.DMA,
            pltpu.SemaphoreType.DMA((2,)),
            pltpu.SemaphoreType.DMA((2,)),
            pltpu.SemaphoreType.DMA((2, cols)),
            pltpu.SemaphoreType.DMA((nchunk, cols)),
            pltpu.SemaphoreType.DMA((2,)),
            pltpu.SemaphoreType.DMA((2,)),
        ],
        compiler_params=pltpu.CompilerParams(
            collective_id=0, has_side_effects=True, vmem_limit_bytes=62 * 1024 * 1024),
        cost_estimate=pl.CostEstimate(
            flops=2 * rows * width * depth * KT, bytes_accessed=8 * rows * width, transcendentals=0),
    )(w, t, live.astype(jnp.float32))
    return out


def solution(mesh):
    placed = (P("row", "col"), P("row", "col"), P("row", None))
    return jax.shard_map(
        functools.partial(body, mesh.shape["row"], mesh.shape["col"]),
        mesh=mesh, in_specs=placed, out_specs=P("row", "col"), check_vma=False)
```

```python
import functools
import heapq
import itertools

import jax
import jax.numpy as jnp
from jax import lax
from jax.experimental import pallas as pl
from jax.experimental.pallas import tpu as pltpu
from jax.sharding import PartitionSpec as P

KT = 8
PIECES = 6
STRETCH = 0.16
BURST = 4
MESH = pl.DeviceIdType.MESH
XD, YD, ZUP, ZDN = 0, 1, 2, 3


def plan(zs_count, group, nchunk, bounds):
    half = PIECES // 2
    dur = [(b - a) / bounds[-1] for a, b in zip(bounds[:-1], bounds[1:])]
    latency = 0.04

    def routes(z, y, x, zz, yy, xx, p):
        outs = []
        onward = [s for s in (-1, 1) if 0 <= z + s < zs_count and s * (z - zz) >= 0]
        if (y, x) == (yy, xx):
            outs = onward + ["x", "y"]
        elif y == yy:
            outs = ["y"] if (p < half if z == zz else p == 0) else []
        elif x == xx:
            outs = ["x"] if (p >= half if z == zz else p == PIECES - 1) else []
        elif 0 < p < PIECES - 1:
            outs = onward
        return outs

    devices = list(itertools.product(range(zs_count), range(2), range(2)))
    count, events, free = itertools.count(), [], {}
    arrivals = {z: [] for z in range(zs_count)}
    for d in devices:
        for p in range(PIECES):
            heapq.heappush(events, (0.0, next(count), d, d, p))
    while events:
        now, _, d, s, p = heapq.heappop(events)
        z, y, x = d
        outs = routes(*d, *s, p)
        if d != s and (y, x) == (0, 0):
            arrivals[z].append((now, s, p, tuple(outs)))
        for link in outs:
            end = max(now, free.get((d, link), 0.0)) + dur[p]
            free[d, link] = end
            to = (z, y, 1 - x) if link == "x" else (z, 1 - y, x) if link == "y" else (z + link, y, x)
            heapq.heappush(events, (end + latency, next(count), to, s, p))
    total = max(a[-1][0] for a in arrivals.values()) + 1e-6
    stretches = int(-(-total // STRETCH))
    order, tiles, ready = [], [], []
    for z in range(zs_count):
        cut = [[] for _ in range(stretches)]
        done = {}
        for now, s, p, outs in arrivals[z]:
            cut[int(now // STRETCH)].append((s, p, outs))
            key = (s[0], s[1] if group == 2 else 0)
            done[key] = max(done.get(key, 0), int(now // STRETCH))
        order.append(cut)
        by_time = sorted(done, key=lambda k: (done[k], abs(k[0] - z), k))
        tiles.append(by_time)
        ready.append([done[k] for k in by_time])
    inner = (KT - 1) * nchunk
    marks = []
    for z in range(zs_count):
        reached = [0]
        for k in range(stretches):
            here = nchunk * sum(r <= k for r in ready[z])
            reached.append(min(here, reached[-1] + BURST, inner))
        marks.append(reached)
    return order, tiles, stretches, marks, inner


def kernel(n, cols, cfg, w_ref, t_ref, live_ref, out_ref, wt_ref,
           tbuf, acc, win, wout, wbuf, obuf,
           recv_sem, send_sem, own_sem, win_sem, wl_sem, ws_sem, wr_sem, wb_sem, o_sem):
    rows, kw, width, kshard, spad, group, chunk, bounds, splits = cfg
    nchunk = rows // chunk
    tiles = kw // (kshard * group)
    zs_count = n // 4
    me = lax.axis_index("row")
    col = lax.axis_index("col")
    x = lax.rem(me, 2)
    y = lax.rem(me // 2, 2)
    z = me // 4
    xo, yo = 1 - x, 1 - y

    def idx(zz, yy, xx):
        return (zz * 2 + yy) * 2 + xx

    target = [(idx(z, y, xo), col), (idx(z, yo, x), col),
              (idx(z + 1, y, x), col), (idx(z - 1, y, x), col)]
    has_up, has_dn = z + 1 < zs_count, z > 0

    barrier = pltpu.get_barrier_semaphore()

    def greet(dev):
        pl.semaphore_signal(barrier, inc=1, device_id=dev, device_id_type=MESH)

    greet(target[XD])
    greet(target[YD])
    pl.when(has_up)(lambda: greet(target[ZUP]))
    pl.when(has_dn)(lambda: greet(target[ZDN]))
    for o in range(1, cols):
        greet((me, lax.rem(col + o, cols)))
    heard = 1 + cols + jnp.where(has_up, 1, 0) + jnp.where(has_dn, 1, 0)
    own = pltpu.make_async_copy(t_ref, tbuf.at[me], own_sem)
    own.start()
    own.wait()
    pl.semaphore_wait(barrier, heard)

    def piece(shard, p):
        return tbuf.at[shard, pl.ds(bounds[p], bounds[p + 1] - bounds[p])]

    def remote(link, shard, p):
        return pltpu.make_async_remote_copy(
            src_ref=piece(shard, p), dst_ref=piece(shard, p),
            send_sem=send_sem.at[link, shard, p], recv_sem=recv_sem.at[shard, p],
            device_id=target[link], device_id_type=MESH)

    def send(go, link, shard, p):
        if go:
            remote(link, shard, p).start()
        else:
            remote(link, shard, p).wait_send()

    def arrive(go, shard, p):
        if go:
            remote(XD, shard, p).wait_recv()

    half = PIECES // 2
    via_z = list(range(1, PIECES - 1))
    via_x, via_y = PIECES - 1, 0

    def own_stage(go):
        for p in range(PIECES):
            send(go, XD, me, p)
            send(go, YD, me, p)
            pl.when(has_up)(functools.partial(send, go, ZUP, me, p))
            pl.when(has_dn)(functools.partial(send, go, ZDN, me, p))

    def onward(go, d, shard, p):
        pl.when((d > 0) & has_dn)(functools.partial(send, go, ZDN, shard, p))
        pl.when((d < 0) & has_up)(functools.partial(send, go, ZUP, shard, p))

    def both(k, work):
        def step(i, carry):
            d = 1 - 2 * i
            zz = z + d * k

            @pl.when((zz >= 0) & (zz < zs_count))
            def _():
                work(d, zz)
            return carry
        lax.fori_loop(0, 2, step, 0)

    def line_stage(go, k):
        def work(d, zz):
            s = idx(zz, y, x)
            for p in range(PIECES):
                arrive(go, s, p)
                onward(go, d, s, p)
                send(go, XD, s, p)
                send(go, YD, s, p)
        both(k, work)

    def diag_stage(go, k):
        def work(d, zz):
            s = idx(zz, yo, xo)
            for p in via_z:
                arrive(go, s, p)
                onward(go, d, s, p)
        both(k, work)

    def side(go, zz, to_y, to_x):
        sx, sy = idx(zz, y, xo), idx(zz, yo, x)
        for p in range(PIECES):
            arrive(go, sx, p)
            if p in to_y:
                send(go, YD, sx, p)
            arrive(go, sy, p)
            if p in to_x:
                send(go, XD, sy, p)

    def side_stage(go, k):
        both(k, lambda d, zz: side(go, zz, (via_y,), (via_x,)))

    def diag_home(go):
        s = idx(z, yo, xo)
        for p in range(PIECES):
            arrive(go, s, p)
            if p in via_z:
                pl.when(has_up)(functools.partial(send, go, ZUP, s, p))
                pl.when(has_dn)(functools.partial(send, go, ZDN, s, p))

    home = (tuple(range(half)), tuple(range(half, PIECES)))

    own_stage(True)

    wout[...] = jnp.zeros_like(wout)

    def w_in(c, slot):
        return pltpu.make_async_copy(w_ref.at[pl.ds(c * chunk, chunk)], win.at[slot], win_sem.at[slot])

    def w_dst(c, owner):
        return wt_ref.at[pl.ds(owner * tiles, tiles), pl.ds(c * chunk, chunk)]

    def w_local(c, slot):
        return pltpu.make_async_copy(wout.at[slot], w_dst(c, col), wl_sem.at[slot])

    def w_remote(c, slot, o):
        return pltpu.make_async_remote_copy(
            src_ref=wout.at[slot], dst_ref=w_dst(c, col),
            send_sem=ws_sem.at[slot, o], recv_sem=wr_sem.at[c, o],
            device_id=(me, lax.rem(col + o, cols)), device_id_type=MESH)

    def w_drain(c, slot):
        w_local(c, slot).wait()
        for o in range(1, cols):
            w_remote(c, slot, o).wait_send()

    w_in(0, 0).start()

    def w_step(c, carry):
        slot = lax.rem(c, 2)
        pl.when(c + 1 < nchunk)(lambda: w_in(c + 1, 1 - slot).start())
        w_in(c, slot).wait()
        pl.when(c >= 2)(lambda: w_drain(c - 2, slot))
        for j in range(tiles):
            for g in range(group):
                at = (j * group + g) * kshard
                wout[slot, j, :, g * spad:g * spad + kshard] = win[slot, :, at:at + kshard]
        w_local(c, slot).start()
        for o in range(1, cols):
            w_remote(c, slot, o).start()
        return carry

    lax.fori_loop(0, nchunk, w_step, 0)

    def w_wait():
        for c in range(max(0, nchunk - 2), nchunk):
            w_drain(c, c % 2)

        def step(c, carry):
            for o in range(1, cols):
                pltpu.make_async_remote_copy(
                    src_ref=wout.at[0], dst_ref=w_dst(c, lax.rem(col + cols - o, cols)),
                    send_sem=ws_sem.at[0, o], recv_sem=wr_sem.at[c, o],
                    device_id=(me, lax.rem(col + o, cols)), device_id_type=MESH).wait_recv()
            return carry
        lax.fori_loop(0, nchunk, step, 0)

    order, tile_order, stretches, marks, inner = plan(zs_count, group, nchunk, bounds)
    total = KT * nchunk

    def tile_at(i):
        t = 0
        for zi in range(zs_count):
            for k, (tz, ty) in enumerate(tile_order[zi]):
                own_y = jnp.where(y == 0, ty, 1 - ty)
                value = tz * 2 + own_y if group == 2 else tz
                t = jnp.where((z == zi) & (i == k), value, t)
        return t

    def fetch(q):
        slot = lax.rem(q, 2)
        return pltpu.make_async_copy(
            wt_ref.at[tile_at(q // nchunk), pl.ds(lax.rem(q, nchunk) * chunk, chunk)],
            wbuf.at[slot], wb_sem.at[slot])

    def store(c, slot):
        return pltpu.make_async_copy(obuf.at[slot], out_ref.at[pl.ds(c * chunk, chunk)], o_sem.at[slot])

    def product(last, q, carry):
        slot, c = lax.rem(q, 2), lax.rem(q, nchunk)
        t = tile_at(q // nchunk)
        live = live_ref[t]
        pl.when(q + 1 < total)(lambda: fetch(q + 1).start())
        fetch(q).wait()
        oslot = lax.rem(c, 2)
        if last:
            pl.when(c >= 2)(lambda: store(c - 2, oslot).wait())
        a = wbuf[slot]
        at = pl.ds(pl.multiple_of(c * chunk, 16), chunk)
        for lo, hi in splits:
            b = tbuf[pl.ds(t * group, group), :, lo:hi].reshape(group * spad, hi - lo)
            d = jnp.dot(a, b, preferred_element_type=jnp.float32) * live
            if last:
                obuf[oslot, :, lo:hi] = (acc[at, lo:hi] + d).astype(jnp.bfloat16)
            else:
                acc[at, lo:hi] += d
        if last:
            store(c, oslot).start()
        return carry

    def clear(c, carry):
        acc[pl.ds(pl.multiple_of(c * chunk, 16), chunk), :] = jnp.zeros((chunk, width), jnp.float32)
        return carry

    lax.fori_loop(0, nchunk, clear, 0)
    w_wait()
    fetch(0).start()

    def relay(events):
        for (sz, sy, sx), p, outs in events:
            shard = idx(sz, y if sy == 0 else yo, x if sx == 0 else xo)
            arrive(True, shard, p)
            for link in outs:
                send(True, {"x": XD, "y": YD, 1: ZUP, -1: ZDN}[link], shard, p)

    def stretch(k, carry):
        for zi in range(zs_count):
            @pl.when(z == zi)
            def _():
                for ki in range(stretches):
                    if order[zi][ki]:
                        pl.when(k == ki)(functools.partial(relay, order[zi][ki]))
        lax.fori_loop(mark(k), mark(k + 1), functools.partial(product, False), 0)
        return carry

    def mark(k):
        value = 0
        for zi in range(zs_count):
            for ki, m in enumerate(marks[zi]):
                if m:
                    value = jnp.where((z == zi) & (k == ki), m, value)
        return value

    lax.fori_loop(0, stretches, stretch, 0)
    lax.fori_loop(mark(stretches), inner, functools.partial(product, False), 0)
    lax.fori_loop(inner, total, functools.partial(product, True), 0)
    for c in range(max(0, nchunk - 2), nchunk):
        store(c, c % 2).wait()

    own_stage(False)
    side(False, z, *home)
    diag_home(False)

    def drain(k, carry):
        line_stage(False, k)
        diag_stage(False, k)
        side_stage(False, k)
        return carry
    lax.fori_loop(1, zs_count, drain, 0)


def body(n, cols, w, t, task_tiles):
    rows, kw = w.shape
    kshard, width = t.shape
    depth = kshard * n // KT
    group = depth // kshard
    spad = -(-kshard // 16) * 16
    chunk = max(c for c in range(16, min(rows, 240) + 1, 16) if rows % c == 0)
    units = spad // 16
    bounds = tuple(units * p // PIECES * 16 for p in range(PIECES + 1))
    parts = max(1, width // 768)
    edges = [768 * i for i in range(parts)] + [width]
    splits = tuple(zip(edges[:-1], edges[1:]))
    tiles = kw // depth
    nchunk = rows // chunk
    tile_ids = jnp.arange(KT, dtype=jnp.int32)
    live = jnp.sum((task_tiles[0][:, None] == tile_ids[None, :]).astype(jnp.int32), axis=0)
    t = jnp.pad(t, ((0, spad - kshard), (0, 0)))
    cfg = (rows, kw, width, kshard, spad, group, chunk, bounds, splits)
    any_space = pl.BlockSpec(memory_space=pl.ANY)
    bf16 = jnp.bfloat16
    out, _ = pl.pallas_call(
        functools.partial(kernel, n, cols, cfg),
        out_shape=(jax.ShapeDtypeStruct((rows, width), bf16),
                   jax.ShapeDtypeStruct((KT, rows, group * spad), bf16)),
        in_specs=[any_space, any_space, pl.BlockSpec(memory_space=pltpu.SMEM)],
        out_specs=(any_space, any_space),
        scratch_shapes=[
            pltpu.VMEM((n, spad, width), bf16),
            pltpu.VMEM((rows, width), jnp.float32),
            pltpu.VMEM((2, chunk, kw), bf16),
            pltpu.VMEM((2, tiles, chunk, group * spad), bf16),
            pltpu.VMEM((2, chunk, group * spad), bf16),
            pltpu.VMEM((2, chunk, width), bf16),
            pltpu.SemaphoreType.DMA((n, PIECES)),
            pltpu.SemaphoreType.DMA((4, n, PIECES)),
            pltpu.SemaphoreType.DMA,
            pltpu.SemaphoreType.DMA((2,)),
            pltpu.SemaphoreType.DMA((2,)),
            pltpu.SemaphoreType.DMA((2, cols)),
            pltpu.SemaphoreType.DMA((nchunk, cols)),
            pltpu.SemaphoreType.DMA((2,)),
            pltpu.SemaphoreType.DMA((2,)),
        ],
        compiler_params=pltpu.CompilerParams(
            collective_id=0, has_side_effects=True, vmem_limit_bytes=62 * 1024 * 1024),
        cost_estimate=pl.CostEstimate(
            flops=2 * rows * width * depth * KT, bytes_accessed=8 * rows * width, transcendentals=0),
    )(w, t, live.astype(jnp.float32))
    return out


def solution(mesh):
    placed = (P("row", "col"), P("row", "col"), P("row", None))
    return jax.shard_map(
        functools.partial(body, mesh.shape["row"], mesh.shape["col"]),
        mesh=mesh, in_specs=placed, out_specs=P("row", "col"), check_vma=False)
```
